32 devices in a mesh: phase: 4 (over x, core), blk: 8 (over z, y).
Axes of the slice: x: 2, y: 2, z: 4, core: 2. Of those that a mesh axis runs over, the one named last changes fastest.
Arguments:
- tokens: bfloat16 [2, 64, 6144], P(None, 'blk'), may hold values from -6 to 6
- norm_gain: float32 [4, 6144], P('phase'), may hold values from 0.5 to 1.5
- up_weight: bfloat16 [4, 6144, 24576], P('phase', None, 'blk'), may hold values from -0.078125 to 0.078125
- up_bias: float32 [4, 24576], P('phase', 'blk'), may hold values from -3 to 3
- down_weight: bfloat16 [4, 24576, 6144], P('phase', 'blk'), may hold values from -0.0390625 to 0.0390625
- down_bias: float32 [4, 6144], P('phase'), may hold values from -3 to 3
Outputs:
- sections: bfloat16 [4, 2, 64, 6144], P('phase', None, 'blk')
The draws below stay inside these ranges and needn't reach their ends.
All inputs are finite; a program needn't handle non-finite values.
Results may differ from the reference program's by a relative error of at most 0.022.
Values may be sent and summed in bfloat16 or wider, within the bound.
No kernel may reach another device: no remote copies, remote signals or barrier semaphores. Data moves between devices by JAX's collectives and lax.ppermute only.
A program may use at most 128 MiB of HBM per device.

```python
import jax
import jax.numpy as jnp
from jax import lax

D = 6144
FF = 24576
MICRO = 2
PHASES = 4
TOKENS = 64
N_BLK = 8


def levels(key, dims, split, smallest, largest):
    level = 1.0
    for dim, blocks in split:
        steps = jax.random.uniform(jax.random.fold_in(jax.random.fold_in(key, 6), dim), (blocks,), jnp.float32, smallest / len(split), largest / len(split))
        level = level * jnp.repeat(jnp.exp(steps), dims[dim] // blocks).reshape((-1,) + (1,) * (len(dims) - 1 - dim))
    return level


def gaussian(own_key, shape, width, reach, split=(), kind=jnp.bfloat16):
    factor_of = levels(own_key, shape, split, -0.22, 0.18) if split else 1.0
    values = jax.random.normal(own_key, shape, jnp.float32) * width * factor_of
    return jnp.minimum(jnp.maximum(values, -reach), reach).astype(kind)


def setup_inputs(seed: int = 0) -> dict:
    keys = jax.random.split(jax.random.key(seed), 7)
    tokens = gaussian(keys[0], (MICRO, TOKENS, D), 1.0, 6.0, ((1, 8),))
    norm_gain = jnp.clip(0.5 + 1.0 * jax.random.uniform(keys[1], (PHASES, D), jnp.float32) ** levels(keys[1], (PHASES, D), ((0, 4),), -0.2, 0.2), 0.5, 1.5)
    up_weight = gaussian(keys[2], (PHASES, D, FF), D ** -0.5, 0.078125, ((0, 4), (2, 8)))
    up_bias = gaussian(keys[3], (PHASES, FF), 0.5, 3.0, ((0, 4), (1, 8)), jnp.float32)
    down_weight = gaussian(keys[4], (PHASES, FF, D), FF ** -0.5, 0.0390625, ((0, 4), (1, 8)))
    down_bias = gaussian(keys[5], (PHASES, D), 0.5, 3.0, ((0, 4),), jnp.float32)
    return {"tokens": tokens, "norm_gain": norm_gain, "up_weight": up_weight, "up_bias": up_bias, "down_weight": down_weight, "down_bias": down_bias}


def section_layer(inputs, gain_row, w_up, b_up, w_down, b_down):
    widened = inputs.astype(jnp.float32)
    row_mean = lax.optimization_barrier(jnp.mean(widened, axis=-1, keepdims=True))
    centered = widened - row_mean
    row_var = lax.optimization_barrier(jnp.mean(centered * centered, axis=-1, keepdims=True))
    normed = (centered * lax.rsqrt(row_var + 1e-05) * gain_row).astype(jnp.bfloat16)
    hidden = jax.nn.gelu(jnp.dot(normed, w_up, preferred_element_type=jnp.float32) + b_up).astype(jnp.bfloat16)
    row_count = hidden.shape[0]
    blocks_hidden = jnp.moveaxis(hidden.reshape(row_count, N_BLK, FF // N_BLK), 1, 0)
    blocks_weight = w_down.reshape(N_BLK, FF // N_BLK, D)

    def accumulate(total, pair):
        part = jnp.dot(pair[0], pair[1], preferred_element_type=jnp.float32).astype(jnp.bfloat16)
        part = lax.optimization_barrier(part)
        return (total + part.astype(jnp.float32), None)
    start_total = jnp.zeros((row_count, D), jnp.float32)
    branch, unused = lax.scan(accumulate, start_total, (blocks_hidden, blocks_weight))
    return (widened + branch + b_down).astype(jnp.bfloat16)

def reference(tokens, norm_gain, up_weight, up_bias, down_weight, down_bias):
    collected = []
    current = [tokens[index] for index in range(MICRO)]
    for level in range(PHASES):
        current = [section_layer(current[index], norm_gain[level], up_weight[level], up_bias[level], down_weight[level], down_bias[level]) for index in range(MICRO)]
        collected.append(jnp.stack(current))
    return jnp.stack(collected)
```

```python
import functools

import jax
import jax.numpy as jnp
from jax import lax
from jax.experimental import pallas as pl
from jax.experimental.pallas import tpu as pltpu
from jax.sharding import PartitionSpec as P

AXES = ("phase", "blk")
ANY = pl.BlockSpec(memory_space=pl.ANY)
VMEM = pl.BlockSpec(memory_space=pltpu.VMEM)
MIB = 1 << 20
SLOTS = 3
SUB = 256


def from_behind(block, axis, distance):
    devices = range(lax.axis_size(axis))
    route = [(i - distance, i) for i in devices if i - distance in devices]
    return lax.ppermute(block, axis, route)


def plain(tokens, norm_gain, up_weight, up_bias, down_weight, down_bias):
    num_micro, num_rows, width = tokens.shape
    phase_index = lax.axis_index("phase")
    num_phases = lax.axis_size("phase")
    inputs = tokens.reshape(num_micro * num_rows, width)
    result = inputs
    for moment in range(num_phases):
        if moment:
            inputs = from_behind(inputs, "phase", 1)
        widened = inputs.astype(jnp.float32)
        centered = widened - jnp.mean(widened, axis=-1, keepdims=True)
        row_var = jnp.mean(centered * centered, axis=-1, keepdims=True)
        normed = (centered * lax.rsqrt(row_var + 1e-05) * norm_gain[0]).astype(jnp.bfloat16)
        gathered = lax.all_gather(normed, "blk", axis=0, tiled=True)
        hidden = jnp.dot(gathered, up_weight[0], preferred_element_type=jnp.float32)
        hidden = jax.nn.gelu(hidden + up_bias[0]).astype(jnp.bfloat16)
        partial = jnp.dot(hidden, down_weight[0], preferred_element_type=jnp.float32)
        branch = lax.psum_scatter(
            partial.astype(jnp.bfloat16), "blk", scatter_dimension=0, tiled=True
        ).astype(jnp.float32)
        inputs = (widened + branch + down_bias[0]).astype(jnp.bfloat16)
        result = jnp.where(phase_index == moment, inputs, result)
    return result.reshape(1, num_micro, num_rows, width)


def fetch_kernel(source, kept, sems):
    parts = sems.shape[0]
    depth = kept.shape[0] // parts
    copies = [
        pltpu.make_async_copy(
            source.at[0, pl.ds(i * depth, depth)], kept.at[pl.ds(i * depth, depth)], sems.at[i]
        )
        for i in range(parts)
    ]
    for copy in copies:
        copy.start()
    for copy in copies:
        copy.wait()


def fetch(up_weight):
    parts = 8
    return pl.pallas_call(
        fetch_kernel,
        out_shape=pltpu.VMEM(up_weight.shape[1:], up_weight.dtype),
        in_specs=[ANY],
        out_specs=VMEM,
        scratch_shapes=[pltpu.SemaphoreType.DMA((parts,))],
        compiler_params=pltpu.CompilerParams(vmem_limit_bytes=MIB),
        cost_estimate=pl.CostEstimate(
            flops=0, bytes_accessed=up_weight.size * 2, transcendentals=0
        ),
    )(up_weight)


def section_kernel(stage, last, n, count, *refs):
    refs = list(refs)
    first = stage == 0
    take = lambda length: [refs.pop(0) for _ in range(length)]
    blocks = take(count)
    gain_row, up_row, down_row, w_up, w_down = take(5)
    if stage > 1:
        take(1)
    sent = take(n)
    kept = None if first else take(1)[0]
    x, normed, hidden, ring, ring_sem, keep_sem = refs
    me = lax.axis_index("blk")
    rows, width = x.shape
    chunk = width // n
    group = rows // n

    def columns(step):
        return pl.ds(pl.multiple_of((me ^ step) * chunk, chunk), chunk)

    def lines(step):
        return pl.ds(pl.multiple_of((me ^ step) * group, group), group)

    def weight_copy(step):
        return pltpu.make_async_copy(
            w_down.at[0, :, columns(step)], ring.at[step % SLOTS], ring_sem.at[step % SLOTS]
        )

    @pl.when(lax.axis_index("phase") == stage)
    def _():
        for step in range(SLOTS):
            weight_copy(step).start()
        for step in range(count):
            if first:
                size = rows // count
                spot = (me // (n // count)) ^ step
                x[pl.ds(pl.multiple_of(spot * size, size), size)] = blocks[step][...]
            else:
                x[:, columns(step)] = blocks[step][...]
        if not first:
            keep = pltpu.make_async_copy(x.at[lines(0)], kept, keep_sem)
            keep.start()

        @pl.loop(0, rows // 16)
        def _(i):
            part = pl.ds(pl.multiple_of(i * 16, 16), 16)
            wide = x[part].astype(jnp.float32)
            centered = wide - jnp.mean(wide, axis=-1, keepdims=True)
            var = jnp.mean(centered * centered, axis=-1, keepdims=True)
            scaled = centered * lax.rsqrt(var + 1e-05) * gain_row[...]
            normed[part] = scaled.astype(jnp.bfloat16)

        for begin in range(0, hidden.shape[1], SUB):
            part = slice(begin, begin + SUB)
            product = jnp.dot(normed[...], w_up[:, part], preferred_element_type=jnp.float32)
            hidden[:, part] = jax.nn.gelu(product + up_row[:, part]).astype(jnp.bfloat16)

        for step in range(n):
            weight_copy(step).wait()
            product = jnp.dot(hidden[...], ring[step % SLOTS], preferred_element_type=jnp.float32)
            if last:
                normed[:, columns(step)] = product.astype(jnp.bfloat16)
            else:
                if step == 0:
                    at = columns(0)
                    product = product + x[:, at].astype(jnp.float32) + down_row[:, at]
                sent[step][...] = product.astype(jnp.bfloat16)
            if step + SLOTS < n:
                weight_copy(step + SLOTS).start()
        if last:
            own = lines(0)
            total = normed[own].astype(jnp.float32) + x[own].astype(jnp.float32) + down_row[...]
            sent[0][...] = total.astype(jnp.bfloat16)
            for step in range(1, n):
                sent[step][...] = normed[lines(step)]
        if not first:
            keep.wait()


def section(stage, last, n, blocks, w_up, gain, b_up, w_down, b_down, kept):
    depth, width = w_down.shape[1:]
    rows = blocks[0].shape[0] * len(blocks) if stage == 0 else blocks[0].shape[0]
    chunk, group = width // n, rows // n
    bf16 = jnp.bfloat16
    shapes = [pltpu.VMEM((group, width) if last else (rows, chunk), bf16)] * n
    near = [*blocks, gain, b_up, b_down, w_up]
    near = [pltpu.with_memory_space_constraint(array, pltpu.VMEM) for array in near]
    operands = [*near, w_down]
    specs = [VMEM] * len(near) + [ANY]
    aliases = {}
    if stage > 0:
        shapes.append(jax.ShapeDtypeStruct((group, width), bf16))
        if kept is not None:
            aliases[len(operands)] = n
            operands.append(kept)
            specs.append(ANY)
    results = pl.pallas_call(
        functools.partial(section_kernel, stage, last, n, len(blocks)),
        out_shape=shapes,
        in_specs=specs,
        out_specs=[VMEM] * n + [ANY] * (len(shapes) - n),
        input_output_aliases=aliases,
        scratch_shapes=[
            pltpu.VMEM((rows, width), bf16),
            pltpu.VMEM((rows, width), bf16),
            pltpu.VMEM((rows, depth), bf16),
            pltpu.VMEM((SLOTS, depth, chunk), bf16),
            pltpu.SemaphoreType.DMA((SLOTS,)),
            pltpu.SemaphoreType.DMA,
        ],
        compiler_params=pltpu.CompilerParams(vmem_limit_bytes=20 * MIB),
        cost_estimate=pl.CostEstimate(
            flops=4 * rows * depth * width,
            bytes_accessed=2 * depth * width,
            transcendentals=rows * depth,
        ),
    )(*operands)
    return results[:n], (results[n] if stage > 0 else None)


HELPER = (2, 3, 1, 2)
STRAIGHT = (((1, 0), (2, 1), (3, 2)), ((0, 2), (1, 3)))


def send(block, source, target, step, n):
    pairs = ((source, target),)
    if step == 0:
        pairs = next((group for group in STRAIGHT if (source, target) in group), pairs)
    return lax.ppermute(block, AXES, [(p * n + b, q * n + (b ^ step)) for p, q in pairs for b in range(n)])


def gather_tokens(mine, n, phases):
    pairwise = [(p * n + b, p * n + (b ^ 1)) for p in range(phases) for b in range(n)]
    other = lax.ppermute(mine, AXES, pairwise)
    odd = lax.rem(lax.axis_index("blk"), 2) == 1
    pair = jnp.concatenate([jnp.where(odd, other, mine), jnp.where(odd, mine, other)])
    return [pair] + [send(pair, 3 - (step - 1) % 3, 0, 2 * step, n) for step in range(1, n // 2)]


def relay(tokens, norm_gain, up_weight, up_bias, down_weight, down_bias):
    num_micro, num_rows, width = tokens.shape
    n = lax.axis_size("blk")
    num_phases = lax.axis_size("phase")
    phase = lax.axis_index("phase")
    blocks = gather_tokens(tokens.reshape(num_micro * num_rows, width), n, num_phases)
    w_up = fetch(up_weight)
    kept = None
    for stage in range(num_phases):
        last = stage == num_phases - 1
        near = HELPER[stage]
        sent, kept = section(
            stage, last, n, blocks, w_up, norm_gain, up_bias, down_weight, down_bias, kept
        )
        landed = [send(sent[step], stage, near, step, n) for step in range(n)]
        total = landed[0].astype(jnp.float32)
        for block in landed[1:]:
            total = total + block.astype(jnp.float32)
        total = total.astype(jnp.bfloat16)
        if not last:
            blocks = [send(total, near, stage + 1, step, n) for step in range(n)]
    earlier = send(kept, 1, 0, 0, n)
    final = send(total, near, stage, 0, n)
    result = jnp.where(phase == num_phases - 1, final, earlier)
    return result.reshape(1, num_micro, num_rows, width)


def fits(mesh, tokens, up_weight):
    n = mesh.shape["blk"]
    num_micro, num_tokens, width = tokens.shape
    depth = up_weight.shape[2] // n
    rows = num_micro * num_tokens
    chunk = width // n
    chunk = width // n
    return (
        mesh.shape["phase"] == 4
        and n & (n - 1) == 0
        and n > SLOTS
        and chunk % 128 == 0
        and depth % SUB == 0
        and (rows // n) % 16 == 0
        and 2 * width * depth <= 36 * MIB
        and 2 * (rows * (2 * width + depth) + SLOTS * depth * chunk) <= 18 * MIB
    )


def solution(mesh):
    def whole(tokens, norm_gain, up_weight, up_bias, down_weight, down_bias):
        body = relay if fits(mesh, tokens, up_weight) else plain
        return jax.shard_map(
            body,
            mesh=mesh,
            in_specs=(
                P(None, "blk", None),
                P("phase", None),
                P("phase", None, "blk"),
                P("phase", "blk"),
                P("phase", "blk", None),
                P("phase", None),
            ),
            out_specs=P("phase", None, "blk", None),
            check_vma=False,
        )(tokens, norm_gain, up_weight, up_bias, down_weight, down_bias)

    return whole
```

```python
import functools

import jax
import jax.numpy as jnp
from jax import lax
from jax.experimental import pallas as pl
from jax.experimental.pallas import tpu as pltpu
from jax.sharding import PartitionSpec as P

AXES = ("phase", "blk")
HBM = pl.BlockSpec(memory_space=pltpu.HBM)
VMEM = pl.BlockSpec(memory_space=pltpu.VMEM)
MIB = 1 << 20
SLOTS = 3
SUB = 512
CUT = 384
STRIP = 256
AHEAD = 1


def from_behind(block, axis, distance):
    devices = range(lax.axis_size(axis))
    route = [(i - distance, i) for i in devices if i - distance in devices]
    return lax.ppermute(block, axis, route)


def plain(tokens, norm_gain, up_weight, up_bias, down_weight, down_bias):
    num_micro, num_rows, width = tokens.shape
    phase_index = lax.axis_index("phase")
    num_phases = lax.axis_size("phase")
    inputs = tokens.reshape(num_micro * num_rows, width)
    result = inputs
    for moment in range(num_phases):
        if moment:
            inputs = from_behind(inputs, "phase", 1)
        widened = inputs.astype(jnp.float32)
        centered = widened - jnp.mean(widened, axis=-1, keepdims=True)
        row_var = jnp.mean(centered * centered, axis=-1, keepdims=True)
        normed = (centered * lax.rsqrt(row_var + 1e-05) * norm_gain[0]).astype(jnp.bfloat16)
        gathered = lax.all_gather(normed, "blk", axis=0, tiled=True)
        hidden = jnp.dot(gathered, up_weight[0], preferred_element_type=jnp.float32)
        hidden = jax.nn.gelu(hidden + up_bias[0]).astype(jnp.bfloat16)
        partial = jnp.dot(hidden, down_weight[0], preferred_element_type=jnp.float32)
        branch = lax.psum_scatter(
            partial.astype(jnp.bfloat16), "blk", scatter_dimension=0, tiled=True
        ).astype(jnp.float32)
        inputs = (widened + branch + down_bias[0]).astype(jnp.bfloat16)
        result = jnp.where(phase_index == moment, inputs, result)
    return result.reshape(1, num_micro, num_rows, width)


def near(*arrays):
    return [pltpu.with_memory_space_constraint(array, pltpu.VMEM) for array in arrays]


def far(array):
    return pltpu.with_memory_space_constraint(array, pltpu.HBM)


def call(kernel, operands, specs, shapes, scratch, megabytes, flops, moved):
    return pl.pallas_call(
        kernel,
        out_shape=shapes,
        in_specs=specs,
        out_specs=[VMEM] * len(shapes),
        scratch_shapes=scratch,
        compiler_params=pltpu.CompilerParams(vmem_limit_bytes=megabytes * MIB),
        cost_estimate=pl.CostEstimate(flops=flops, bytes_accessed=moved, transcendentals=0),
    )(*operands)


def part_of(index, size):
    return pl.ds(pl.multiple_of(index * size, size), size)


def fetch_kernel(n, w_down, *refs):
    kept, sems = refs[:n], refs[n]
    me = lax.axis_index("blk")
    copies = [
        pltpu.make_async_copy(
            w_down.at[0, :, part_of(me ^ order(i, n), kept[i].shape[1])], kept[i], sems.at[i]
        )
        for i in range(n)
    ]
    for copy in copies:
        copy.start()
    for copy in copies:
        copy.wait()


def fetch(n, w_down):
    depth, width = w_down.shape[1:]
    return call(
        functools.partial(fetch_kernel, n),
        (far(w_down),),
        [HBM],
        [pltpu.VMEM((depth, width // n), w_down.dtype)] * n,
        [pltpu.SemaphoreType.DMA((n,))],
        1,
        0,
        2 * width * depth,
    )


def first_kernel(n, *refs):
    blocks = refs[:n]
    gain, b_up, w_up, hidden, own, x, normed, ring, sems = refs[n:]
    me = lax.axis_index("blk")
    rows, width = x.shape
    group = rows // n
    parts = hidden.shape[1] // STRIP

    def weight_copy(i):
        slot = lax.rem(i, SLOTS)
        return pltpu.make_async_copy(
            w_up.at[0, :, part_of(i, STRIP)], ring.at[slot], sems.at[slot]
        )

    @pl.when(lax.axis_index("phase") == 0)
    def _():
        for i in range(SLOTS):
            weight_copy(jnp.int32(i)).start()
        for i in range(n):
            x[part_of(me ^ token_order(i, n), group)] = blocks[i][...]
        own[...] = x[:, part_of(me, own.shape[1])]

        @pl.loop(0, rows // 16)
        def _(i):
            part = part_of(i, 16)
            wide = x[part].astype(jnp.float32)
            centered = wide - jnp.mean(wide, axis=-1, keepdims=True)
            var = jnp.mean(centered * centered, axis=-1, keepdims=True)
            scaled = centered * lax.rsqrt(var + 1e-05) * gain[...]
            normed[part] = scaled.astype(jnp.bfloat16)

        @pl.loop(0, parts)
        def _(i):
            weight_copy(i).wait()
            part = part_of(i, STRIP)
            product = jnp.dot(
                normed[...], ring[lax.rem(i, SLOTS)], preferred_element_type=jnp.float32
            )
            hidden[:, part] = jax.nn.gelu(product + b_up[:, part]).astype(jnp.bfloat16)

            @pl.when(i + SLOTS < parts)
            def _():
                weight_copy(i + SLOTS).start()


def first_hidden(n, blocks, gain, b_up, w_up):
    width, depth = w_up.shape[1:]
    rows = blocks[0].shape[0] * n
    return call(
        functools.partial(first_kernel, n),
        (*near(*blocks, gain, b_up), far(w_up)),
        [VMEM] * (n + 2) + [HBM],
        [
            pltpu.VMEM((rows, depth), jnp.bfloat16),
            pltpu.VMEM((rows, width // n), jnp.bfloat16),
        ],
        [
            pltpu.VMEM((rows, width), jnp.bfloat16),
            pltpu.VMEM((rows, width), jnp.bfloat16),
            pltpu.VMEM((SLOTS, width, STRIP), jnp.bfloat16),
            pltpu.SemaphoreType.DMA((SLOTS,)),
        ],
        13,
        2 * rows * width * depth,
        2 * width * depth,
    )


def weight_copies(first, n, w_up, targets, sems):
    me = lax.axis_index("blk")
    chunk = targets[0].shape[0]
    cuts = chunk // CUT
    return [
        pltpu.make_async_copy(
            w_up.at[0, part_of((me ^ arrival(first + i, n)) * cuts + t, CUT)],
            target.at[pl.ds(t * CUT, CUT)],
            sems.at[i * cuts + t],
        )
        for i, target in enumerate(targets)
        for t in range(cuts)
    ]


def ahead_kernel(stage, n, w_up, *refs):
    *targets, sems = refs

    @pl.when(lax.axis_index("phase") == stage)
    def _():
        copies = weight_copies(0, n, w_up, targets, sems)
        for copy in copies:
            copy.start()
        for copy in copies:
            copy.wait()


def ahead(stage, n, w_up):
    width, depth = w_up.shape[1:]
    chunk = width // n
    return call(
        functools.partial(ahead_kernel, stage, n),
        (far(w_up),),
        [HBM],
        [pltpu.VMEM((chunk, depth), w_up.dtype)] * AHEAD,
        [pltpu.SemaphoreType.DMA((AHEAD * chunk // CUT,))],
        1,
        0,
        2 * AHEAD * chunk * depth,
    )


def up_kernel(stage, i, n, *refs):
    refs = list(refs)
    take = lambda length: [refs.pop(0) for _ in range(length)]
    first, last = i == 0, i == n - 1
    block, gain, weights = take(3)
    before, seen = (None, None) if first else take(2)
    fetches = i + AHEAD < n
    b_up = take(1)[0] if last else None
    w_up = take(1)[0] if fetches else None
    if last:
        hidden, scaled = refs
    else:
        total, noted, *refs = refs
        following = refs[:1] if fetches else []
        scaled = refs[len(following)]
    rows, chunk = block.shape
    depth = weights.shape[1]

    @pl.when(lax.axis_index("phase") == stage)
    def _():
        copies = weight_copies(i + AHEAD, n, w_up, following, refs[-1]) if fetches else []
        for copy in copies:
            copy.start()
        row = gain[:, part_of(lax.axis_index("blk") ^ arrival(i, n), chunk)]
        wide = block[...].astype(jnp.float32)
        shift = jnp.mean(wide, axis=-1, keepdims=True) if first else seen[0, :, :1]
        moved = wide - shift
        scaled[:rows] = (moved * row).astype(jnp.bfloat16)
        scaled[rows:] = jnp.broadcast_to(row, (16, chunk)).astype(jnp.bfloat16)
        one = jnp.sum(moved, axis=-1, keepdims=True)
        two = jnp.sum(moved * moved, axis=-1, keepdims=True)
        if not first:
            one = one + seen[1, :, :1]
            two = two + seen[2, :, :1]
        if not last:
            for t, value in enumerate((shift, one, two)):
                noted[t] = jnp.broadcast_to(value, (rows, 128))
        mean = one / (n * chunk)
        scale = lax.rsqrt(two / (n * chunk) - mean * mean + 1e-05)

        @pl.loop(0, depth // SUB, unroll=3)
        def _(c):
            part = part_of(c, SUB)
            product = jnp.dot(scaled[...], weights[:, part], preferred_element_type=jnp.float32)
            if not first:
                product = before[:, part] + product
            if last:
                product = (product[:rows] - mean * product[rows : rows + 1]) * scale
                hidden[:, part] = jax.nn.gelu(product + b_up[:, part]).astype(jnp.bfloat16)
            else:
                total[:, part] = product

        for copy in copies:
            copy.wait()


def next_hidden(stage, n, blocks, gain, b_up, w_up, weights):
    depth = w_up.shape[2]
    rows, chunk = blocks[0].shape
    total = (rows + 16, depth)
    carried = []
    for i in range(n):
        last, fetches = i == n - 1, i + AHEAD < n
        operands = near(blocks[i], gain, weights[i], *carried, *([b_up] if last else []))
        results = call(
            functools.partial(up_kernel, stage, i, n),
            [*operands, far(w_up)] if fetches else operands,
            [VMEM] * len(operands) + [HBM] * fetches,
            [pltpu.VMEM((rows, depth), jnp.bfloat16)]
            if last
            else [
                pltpu.VMEM(total, jnp.float32),
                pltpu.VMEM((3, rows, 128), jnp.float32),
                *[pltpu.VMEM((chunk, depth), jnp.bfloat16)] * fetches,
            ],
            [pltpu.VMEM((rows + 16, chunk), jnp.bfloat16)]
            + [pltpu.SemaphoreType.DMA((chunk // CUT,))] * fetches,
            3,
            2 * rows * chunk * depth,
            2 * chunk * depth,
        )
        carried = results[:2]
        weights = [*weights, *results[2:]]
    return results[0]


def down_kernel(stage, hidden, weights, *refs):
    sent = refs[-1]

    @pl.when(lax.axis_index("phase") == stage)
    def _():
        product = jnp.dot(hidden[...], weights[...], preferred_element_type=jnp.float32)
        if len(refs) > 1:
            x, b_down, _ = refs
            columns = part_of(lax.axis_index("blk"), sent.shape[1])
            product = product + x[...].astype(jnp.float32) + b_down[:, columns]
        sent[...] = product.astype(jnp.bfloat16)


def down(stage, hidden, weights, own, b_down):
    rows, depth = hidden.shape
    chunk = weights.shape[1]
    operands = [hidden, weights] + ([] if own is None else [own, b_down])
    return call(
        functools.partial(down_kernel, stage),
        near(*operands),
        [VMEM] * len(operands),
        [pltpu.VMEM((rows, chunk), jnp.bfloat16)],
        [],
        2,
        2 * rows * depth * chunk,
        2 * depth * chunk,
    )[0]


def last_kernel(stage, n, hidden, x, b_down, *refs):
    weights, sent, whole = refs[:n], refs[n : 2 * n], refs[2 * n]
    me = lax.axis_index("blk")
    chunk = weights[0].shape[1]
    group = x.shape[0]

    @pl.when(lax.axis_index("phase") == stage)
    def _():
        for i in range(n):
            product = jnp.dot(hidden[...], weights[i][...], preferred_element_type=jnp.float32)
            whole[:, part_of(me ^ order(i, n), chunk)] = product.astype(jnp.bfloat16)
        for i in range(n):
            part = whole[part_of(me ^ order(i, n), group)]
            if order(i, n) == 0:
                part = part.astype(jnp.float32) + x[...].astype(jnp.float32) + b_down[...]
            sent[i][...] = part.astype(jnp.bfloat16)


def last_down(stage, n, hidden, down_kept, own, b_down):
    rows, depth = hidden.shape
    group, width = own.shape
    return call(
        functools.partial(last_kernel, stage, n),
        near(hidden, own, b_down, *down_kept),
        [VMEM] * (n + 3),
        [pltpu.VMEM((group, width), jnp.bfloat16)] * n,
        [pltpu.VMEM((rows, width), jnp.bfloat16)],
        4,
        2 * rows * depth * width,
        2 * depth * width,
    )


def rows_kernel(stage, n, *refs):
    blocks, own = refs[:n], refs[-1]
    me = lax.axis_index("blk")
    group = own.shape[0]
    chunk = blocks[0].shape[1]

    if stage > 1:

        @pl.when(lax.axis_index("phase") != stage)
        def _():
            own[...] = refs[n][...]

    @pl.when(lax.axis_index("phase") == stage)
    def _():
        for i in range(n):
            own[:, part_of(me ^ arrival(i, n), chunk)] = blocks[i][part_of(me, group)]


def own_rows(stage, n, blocks, kept):
    rows, chunk = blocks[0].shape
    operands = [*blocks] + ([kept] if stage > 1 else [])
    return call(
        functools.partial(rows_kernel, stage, n),
        near(*operands),
        [VMEM] * len(operands),
        [pltpu.VMEM((rows // n, chunk * n), jnp.bfloat16)],
        [],
        1,
        0,
        4 * rows * chunk,
    )[0]


def order(i, n):
    half = n // 2
    return (half + (i + 1) // 2 if i % 2 or i == 0 else i // 2) % n


def token_order(i, n):
    half = n // 2
    return (i + 1) // 2 % half if i % 2 else i // 2 + half


def arrival(i, n):
    half = n // 2
    return (0, 1, half, half + 1)[i] if i < 4 else i // 2 + (half if i % 2 else 0)


def send(block, source, target, step, n, phases):
    pairs = ((source, target),)
    if source ^ 1 == target:
        pairs = [(p, p ^ 1) for p in range(source % 2, phases, 2)]
    return lax.ppermute(block, AXES, [(p * n + b, q * n + (b ^ step)) for p, q in pairs for b in range(n)])


def relay(tokens, norm_gain, up_weight, up_bias, down_weight, down_bias):
    num_micro, num_rows, width = tokens.shape
    n = lax.axis_size("blk")
    num_phases = lax.axis_size("phase")
    phase = lax.axis_index("phase")
    steps = [order(i, n) for i in range(n)]
    mine = tokens.reshape(num_micro * num_rows, width)
    blocks = [token_order(i, n) for i in range(n)]
    blocks = [send(mine, 1, 0, step, n, num_phases) if step else mine for step in blocks]
    down_kept = fetch(n, down_weight)
    kept = None
    for stage in range(num_phases):
        last = stage == num_phases - 1
        adder = stage ^ 1
        turns = [*range(n)]
        if stage == 0:
            turns = [*turns[n // 2 : n - 1], *turns[: n // 2], n - 1]
        if stage == 0:
            hidden, own = first_hidden(n, blocks, norm_gain, up_bias, up_weight)
        else:
            hidden = next_hidden(stage, n, blocks, norm_gain, up_bias, up_weight, early)
            kept = own_rows(stage, n, blocks, kept)
            own = blocks[0]
        if last:
            sent = last_down(stage, n, hidden, down_kept, kept, down_bias)
        else:
            sent = [
                down(stage, hidden, down_kept[i], None if steps[i] else own, down_bias)
                for i in turns
            ]
        landed = [send(sent[k], stage, adder, steps[i], n, num_phases) for k, i in enumerate(turns)]
        total = landed[0].astype(jnp.float32)
        for block in landed[1:]:
            total = total + block.astype(jnp.float32)
        total = total.astype(jnp.bfloat16)
        if not last:
            sender = (stage + 1) ^ 1
            total = send(total, adder, sender, 0, n, num_phases)
            early = ahead(stage + 1, n, up_weight)
            blocks = {step: send(total, sender, stage + 1, step, n, num_phases) for step in steps}
            blocks = [blocks[arrival(i, n)] for i in range(n)]
    straight = send(kept, 1, 0, 0, n, num_phases)
    across = send(kept, 2, 1, 0, n, num_phases)
    final = send(total, adder, stage, 0, n, num_phases)
    result = jnp.where(phase == stage, final, jnp.where(phase == 1, across, straight))
    return result.reshape(1, num_micro, num_rows, width)


def fits(mesh, tokens, up_weight):
    n = mesh.shape["blk"]
    num_micro, num_tokens, width = tokens.shape
    depth = up_weight.shape[2] // n
    rows = num_micro * num_tokens
    chunk = width // n
    chunk = width // n
    return (
        mesh.shape["phase"] == 4
        and n & (n - 1) == 0
        and n >= 4
        and chunk % CUT == 0
        and depth % SUB == 0
        and depth % STRIP == 0
        and (rows // n) % 16 == 0
        and 2 * depth * (width + (AHEAD + 1) * chunk) <= 50 * MIB
        and 4 * rows * width + 2 * SLOTS * width * STRIP <= 12 * MIB
        and 4 * rows * depth <= 2 * MIB
    )


def solution(mesh):
    def whole(tokens, norm_gain, up_weight, up_bias, down_weight, down_bias):
        body = relay if fits(mesh, tokens, up_weight) else plain
        return jax.shard_map(
            body,
            mesh=mesh,
            in_specs=(
                P(None, "blk", None),
                P("phase", None),
                P("phase", None, "blk"),
                P("phase", "blk"),
                P("phase", "blk", None),
                P("phase", None),
            ),
            out_specs=P("phase", None, "blk", None),
            check_vma=False,
        )(tokens, norm_gain, up_weight, up_bias, down_weight, down_bias)

    return whole
```

```python
import functools

import jax
import jax.numpy as jnp
from jax import lax
from jax.experimental import pallas as pl
from jax.experimental.pallas import tpu as pltpu
from jax.sharding import PartitionSpec as P

AXES = ("phase", "blk")
HBM = pl.BlockSpec(memory_space=pltpu.HBM)
VMEM = pl.BlockSpec(memory_space=pltpu.VMEM)
MIB = 1 << 20
SLOTS = 3
SUB = 512
CUT = 384
STRIP = 256
AHEAD = 1


def from_behind(block, axis, distance):
    devices = range(lax.axis_size(axis))
    route = [(i - distance, i) for i in devices if i - distance in devices]
    return lax.ppermute(block, axis, route)


def plain(tokens, norm_gain, up_weight, up_bias, down_weight, down_bias):
    num_micro, num_rows, width = tokens.shape
    phase_index = lax.axis_index("phase")
    num_phases = lax.axis_size("phase")
    inputs = tokens.reshape(num_micro * num_rows, width)
    result = inputs
    for moment in range(num_phases):
        if moment:
            inputs = from_behind(inputs, "phase", 1)
        widened = inputs.astype(jnp.float32)
        centered = widened - jnp.mean(widened, axis=-1, keepdims=True)
        row_var = jnp.mean(centered * centered, axis=-1, keepdims=True)
        normed = (centered * lax.rsqrt(row_var + 1e-05) * norm_gain[0]).astype(jnp.bfloat16)
        gathered = lax.all_gather(normed, "blk", axis=0, tiled=True)
        hidden = jnp.dot(gathered, up_weight[0], preferred_element_type=jnp.float32)
        hidden = jax.nn.gelu(hidden + up_bias[0]).astype(jnp.bfloat16)
        partial = jnp.dot(hidden, down_weight[0], preferred_element_type=jnp.float32)
        branch = lax.psum_scatter(
            partial.astype(jnp.bfloat16), "blk", scatter_dimension=0, tiled=True
        ).astype(jnp.float32)
        inputs = (widened + branch + down_bias[0]).astype(jnp.bfloat16)
        result = jnp.where(phase_index == moment, inputs, result)
    return result.reshape(1, num_micro, num_rows, width)


def near(*arrays):
    return [pltpu.with_memory_space_constraint(array, pltpu.VMEM) for array in arrays]


def far(array):
    return pltpu.with_memory_space_constraint(array, pltpu.HBM)


def call(kernel, operands, specs, shapes, scratch, megabytes, flops, moved):
    return pl.pallas_call(
        kernel,
        out_shape=shapes,
        in_specs=specs,
        out_specs=[VMEM] * len(shapes),
        scratch_shapes=scratch,
        compiler_params=pltpu.CompilerParams(vmem_limit_bytes=megabytes * MIB),
        cost_estimate=pl.CostEstimate(flops=flops, bytes_accessed=moved, transcendentals=0),
    )(*operands)


def part_of(index, size):
    return pl.ds(pl.multiple_of(index * size, size), size)


def fetch_kernel(n, w_down, *refs):
    kept, sems = refs[:n], refs[n]
    me = lax.axis_index("blk")
    copies = [
        pltpu.make_async_copy(
            w_down.at[0, :, part_of(me ^ order(i, n), kept[i].shape[1])], kept[i], sems.at[i]
        )
        for i in range(n)
    ]
    for copy in copies:
        copy.start()
    for copy in copies:
        copy.wait()


def fetch(n, w_down):
    depth, width = w_down.shape[1:]
    return call(
        functools.partial(fetch_kernel, n),
        (far(w_down),),
        [HBM],
        [pltpu.VMEM((depth, width // n), w_down.dtype)] * n,
        [pltpu.SemaphoreType.DMA((n,))],
        1,
        0,
        2 * width * depth,
    )


def first_kernel(n, *refs):
    blocks = refs[:n]
    gain, b_up, w_up, hidden, own, x, normed, ring, sems = refs[n:]
    me = lax.axis_index("blk")
    rows, width = x.shape
    group = rows // n
    parts = hidden.shape[1] // STRIP

    def weight_copy(i):
        slot = lax.rem(i, SLOTS)
        return pltpu.make_async_copy(
            w_up.at[0, :, part_of(i, STRIP)], ring.at[slot], sems.at[slot]
        )

    @pl.when(lax.axis_index("phase") == 0)
    def _():
        for i in range(SLOTS):
            weight_copy(jnp.int32(i)).start()
        for i in range(n):
            x[part_of(me ^ order(i, n), group)] = blocks[i][...]
        own[...] = x[:, part_of(me, own.shape[1])]

        @pl.loop(0, rows // 16)
        def _(i):
            part = part_of(i, 16)
            wide = x[part].astype(jnp.float32)
            centered = wide - jnp.mean(wide, axis=-1, keepdims=True)
            var = jnp.mean(centered * centered, axis=-1, keepdims=True)
            scaled = centered * lax.rsqrt(var + 1e-05) * gain[...]
            normed[part] = scaled.astype(jnp.bfloat16)

        @pl.loop(0, parts)
        def _(i):
            weight_copy(i).wait()
            part = part_of(i, STRIP)
            product = jnp.dot(
                normed[...], ring[lax.rem(i, SLOTS)], preferred_element_type=jnp.float32
            )
            hidden[:, part] = jax.nn.gelu(product + b_up[:, part]).astype(jnp.bfloat16)

            @pl.when(i + SLOTS < parts)
            def _():
                weight_copy(i + SLOTS).start()


def first_hidden(n, blocks, gain, b_up, w_up):
    width, depth = w_up.shape[1:]
    rows = blocks[0].shape[0] * n
    return call(
        functools.partial(first_kernel, n),
        (*near(*blocks, gain, b_up), far(w_up)),
        [VMEM] * (n + 2) + [HBM],
        [
            pltpu.VMEM((rows, depth), jnp.bfloat16),
            pltpu.VMEM((rows, width // n), jnp.bfloat16),
        ],
        [
            pltpu.VMEM((rows, width), jnp.bfloat16),
            pltpu.VMEM((rows, width), jnp.bfloat16),
            pltpu.VMEM((SLOTS, width, STRIP), jnp.bfloat16),
            pltpu.SemaphoreType.DMA((SLOTS,)),
        ],
        13,
        2 * rows * width * depth,
        2 * width * depth,
    )


def weight_copies(first, n, w_up, targets, sems):
    me = lax.axis_index("blk")
    chunk = targets[0].shape[0]
    cuts = chunk // CUT
    return [
        pltpu.make_async_copy(
            w_up.at[0, part_of((me ^ arrival(first + i, n)) * cuts + t, CUT)],
            target.at[pl.ds(t * CUT, CUT)],
            sems.at[i * cuts + t],
        )
        for i, target in enumerate(targets)
        for t in range(cuts)
    ]


def ahead_kernel(stage, n, w_up, *refs):
    *targets, sems = refs

    @pl.when(lax.axis_index("phase") == stage)
    def _():
        copies = weight_copies(0, n, w_up, targets, sems)
        for copy in copies:
            copy.start()
        for copy in copies:
            copy.wait()


def ahead(stage, n, w_up):
    width, depth = w_up.shape[1:]
    chunk = width // n
    return call(
        functools.partial(ahead_kernel, stage, n),
        (far(w_up),),
        [HBM],
        [pltpu.VMEM((chunk, depth), w_up.dtype)] * AHEAD,
        [pltpu.SemaphoreType.DMA((AHEAD * chunk // CUT,))],
        1,
        0,
        2 * AHEAD * chunk * depth,
    )


def up_kernel(stage, i, n, *refs):
    refs = list(refs)
    take = lambda length: [refs.pop(0) for _ in range(length)]
    first, last = i == 0, i == n - 1
    block, gain, weights = take(3)
    before, seen = (None, None) if first else take(2)
    fetches = i + AHEAD < n
    b_up = take(1)[0] if last else None
    w_up = take(1)[0] if fetches else None
    if last:
        hidden, scaled = refs
    else:
        total, noted, *refs = refs
        following = refs[:1] if fetches else []
        scaled = refs[len(following)]
    rows, chunk = block.shape
    depth = weights.shape[1]

    @pl.when(lax.axis_index("phase") == stage)
    def _():
        copies = weight_copies(i + AHEAD, n, w_up, following, refs[-1]) if fetches else []
        for copy in copies:
            copy.start()
        row = gain[:, part_of(lax.axis_index("blk") ^ arrival(i, n), chunk)]
        wide = block[...].astype(jnp.float32)
        shift = jnp.mean(wide, axis=-1, keepdims=True) if first else seen[0, :, :1]
        moved = wide - shift
        scaled[:rows] = (moved * row).astype(jnp.bfloat16)
        scaled[rows:] = jnp.broadcast_to(row, (16, chunk)).astype(jnp.bfloat16)
        one = jnp.sum(moved, axis=-1, keepdims=True)
        two = jnp.sum(moved * moved, axis=-1, keepdims=True)
        if not first:
            one = one + seen[1, :, :1]
            two = two + seen[2, :, :1]
        if not last:
            for t, value in enumerate((shift, one, two)):
                noted[t] = jnp.broadcast_to(value, (rows, 128))
        mean = one / (n * chunk)
        scale = lax.rsqrt(two / (n * chunk) - mean * mean + 1e-05)

        @pl.loop(0, depth // SUB, unroll=3)
        def _(c):
            part = part_of(c, SUB)
            product = jnp.dot(scaled[...], weights[:, part], preferred_element_type=jnp.float32)
            if not first:
                product = before[:, part] + product
            if last:
                product = (product[:rows] - mean * product[rows : rows + 1]) * scale
                hidden[:, part] = jax.nn.gelu(product + b_up[:, part]).astype(jnp.bfloat16)
            else:
                total[:, part] = product

        for copy in copies:
            copy.wait()


def next_hidden(stage, n, blocks, gain, b_up, w_up, weights):
    depth = w_up.shape[2]
    rows, chunk = blocks[0].shape
    total = (rows + 16, depth)
    carried = []
    for i in range(n):
        last, fetches = i == n - 1, i + AHEAD < n
        operands = near(blocks[i], gain, weights[i], *carried, *([b_up] if last else []))
        results = call(
            functools.partial(up_kernel, stage, i, n),
            [*operands, far(w_up)] if fetches else operands,
            [VMEM] * len(operands) + [HBM] * fetches,
            [pltpu.VMEM((rows, depth), jnp.bfloat16)]
            if last
            else [
                pltpu.VMEM(total, jnp.float32),
                pltpu.VMEM((3, rows, 128), jnp.float32),
                *[pltpu.VMEM((chunk, depth), jnp.bfloat16)] * fetches,
            ],
            [pltpu.VMEM((rows + 16, chunk), jnp.bfloat16)]
            + [pltpu.SemaphoreType.DMA((chunk // CUT,))] * fetches,
            3,
            2 * rows * chunk * depth,
            2 * chunk * depth,
        )
        carried = results[:2]
        weights = [*weights, *results[2:]]
    return results[0]


def down_kernel(stage, hidden, weights, *refs):
    sent = refs[-1]

    @pl.when(lax.axis_index("phase") == stage)
    def _():
        product = jnp.dot(hidden[...], weights[...], preferred_element_type=jnp.float32)
        if len(refs) > 1:
            x, b_down, _ = refs
            columns = part_of(lax.axis_index("blk"), sent.shape[1])
            product = product + x[...].astype(jnp.float32) + b_down[:, columns]
        sent[...] = product.astype(jnp.bfloat16)


def down(stage, hidden, weights, own, b_down):
    rows, depth = hidden.shape
    chunk = weights.shape[1]
    operands = [hidden, weights] + ([] if own is None else [own, b_down])
    return call(
        functools.partial(down_kernel, stage),
        near(*operands),
        [VMEM] * len(operands),
        [pltpu.VMEM((rows, chunk), jnp.bfloat16)],
        [],
        2,
        2 * rows * depth * chunk,
        2 * depth * chunk,
    )[0]


def last_kernel(stage, n, hidden, x, b_down, *refs):
    weights, sent, whole = refs[:n], refs[n : 2 * n], refs[2 * n]
    me = lax.axis_index("blk")
    chunk = weights[0].shape[1]
    group = x.shape[0]

    @pl.when(lax.axis_index("phase") == stage)
    def _():
        for i in range(n):
            product = jnp.dot(hidden[...], weights[i][...], preferred_element_type=jnp.float32)
            whole[:, part_of(me ^ order(i, n), chunk)] = product.astype(jnp.bfloat16)
        for i in range(n):
            part = whole[part_of(me ^ order(i, n), group)]
            if order(i, n) == 0:
                part = part.astype(jnp.float32) + x[...].astype(jnp.float32) + b_down[...]
            sent[i][...] = part.astype(jnp.bfloat16)


def last_down(stage, n, hidden, down_kept, own, b_down):
    rows, depth = hidden.shape
    group, width = own.shape
    return call(
        functools.partial(last_kernel, stage, n),
        near(hidden, own, b_down, *down_kept),
        [VMEM] * (n + 3),
        [pltpu.VMEM((group, width), jnp.bfloat16)] * n,
        [pltpu.VMEM((rows, width), jnp.bfloat16)],
        4,
        2 * rows * depth * width,
        2 * depth * width,
    )


def rows_kernel(stage, n, *refs):
    blocks, own = refs[:n], refs[-1]
    me = lax.axis_index("blk")
    group = own.shape[0]
    chunk = blocks[0].shape[1]

    if stage > 1:

        @pl.when(lax.axis_index("phase") != stage)
        def _():
            own[...] = refs[n][...]

    @pl.when(lax.axis_index("phase") == stage)
    def _():
        for i in range(n):
            own[:, part_of(me ^ arrival(i, n), chunk)] = blocks[i][part_of(me, group)]


def own_rows(stage, n, blocks, kept):
    rows, chunk = blocks[0].shape
    operands = [*blocks] + ([kept] if stage > 1 else [])
    return call(
        functools.partial(rows_kernel, stage, n),
        near(*operands),
        [VMEM] * len(operands),
        [pltpu.VMEM((rows // n, chunk * n), jnp.bfloat16)],
        [],
        1,
        0,
        4 * rows * chunk,
    )[0]


def order(i, n):
    half = n // 2
    return (i + 1) // 2 % half if i % 2 else i // 2 + half


def arrival(i, n):
    half = n // 2
    return (0, 1, half, half + 1)[i] if i < 4 else i // 2 + (half if i % 2 else 0)


def send(block, source, target, step, n, phases):
    pairs = ((source, target),)
    if source ^ 1 == target:
        pairs = [(p, p ^ 1) for p in range(source % 2, phases, 2)]
    return lax.ppermute(block, AXES, [(p * n + b, q * n + (b ^ step)) for p, q in pairs for b in range(n)])


def relay(tokens, norm_gain, up_weight, up_bias, down_weight, down_bias):
    num_micro, num_rows, width = tokens.shape
    n = lax.axis_size("blk")
    num_phases = lax.axis_size("phase")
    phase = lax.axis_index("phase")
    steps = [order(i, n) for i in range(n)]
    mine = tokens.reshape(num_micro * num_rows, width)
    blocks = [order(i, n) for i in range(n)]
    blocks = [send(mine, 1, 0, step, n, num_phases) if step else mine for step in blocks]
    down_kept = fetch(n, down_weight)
    kept = None
    for stage in range(num_phases):
        last = stage == num_phases - 1
        adder = stage ^ 1
        turns = [*range(n)]
        if stage == 0:
            turns[3 : n - 1] = [i for k in range(4, n - 1, 2) for i in (k, k - 1)]
            turns = [*turns[4 : n - 1], *turns[:4], n - 1]
        if stage == 0:
            hidden, own = first_hidden(n, blocks, norm_gain, up_bias, up_weight)
        else:
            hidden = next_hidden(stage, n, blocks, norm_gain, up_bias, up_weight, early)
            kept = own_rows(stage, n, blocks, kept)
            own = blocks[0]
        if last:
            sent = last_down(stage, n, hidden, down_kept, kept, down_bias)
        else:
            sent = [
                down(stage, hidden, down_kept[i], None if steps[i] else own, down_bias)
                for i in turns
            ]
        landed = [send(sent[k], stage, adder, steps[i], n, num_phases) for k, i in enumerate(turns)]
        total = landed[0].astype(jnp.float32)
        for block in landed[1:]:
            total = total + block.astype(jnp.float32)
        total = total.astype(jnp.bfloat16)
        if not last:
            own = total if adder == stage + 1 else send(total, adder, stage + 1, 0, n, num_phases)
            sender = (stage + 1) ^ 1
            total = send(total, adder, sender, 0, n, num_phases)
            early = ahead(stage + 1, n, up_weight)
            blocks = {step: send(total, sender, stage + 1, step, n, num_phases) for step in steps if step}
            blocks[0] = own
            blocks = [blocks[arrival(i, n)] for i in range(n)]
    straight = send(kept, 1, 0, 0, n, num_phases)
    across = send(kept, 2, 1, 0, n, num_phases)
    final = send(total, adder, stage, 0, n, num_phases)
    result = jnp.where(phase == stage, final, jnp.where(phase == 1, across, straight))
    return result.reshape(1, num_micro, num_rows, width)


def fits(mesh, tokens, up_weight):
    n = mesh.shape["blk"]
    num_micro, num_tokens, width = tokens.shape
    depth = up_weight.shape[2] // n
    rows = num_micro * num_tokens
    chunk = width // n
    chunk = width // n
    return (
        mesh.shape["phase"] == 4
        and n & (n - 1) == 0
        and n >= 4
        and chunk % CUT == 0
        and depth % SUB == 0
        and depth % STRIP == 0
        and (rows // n) % 16 == 0
        and 2 * depth * (width + (AHEAD + 1) * chunk) <= 50 * MIB
        and 4 * rows * width + 2 * SLOTS * width * STRIP <= 12 * MIB
        and 4 * rows * depth <= 2 * MIB
    )


def solution(mesh):
    def whole(tokens, norm_gain, up_weight, up_bias, down_weight, down_bias):
        body = relay if fits(mesh, tokens, up_weight) else plain
        return jax.shard_map(
            body,
            mesh=mesh,
            in_specs=(
                P(None, "blk", None),
                P("phase", None),
                P("phase", None, "blk"),
                P("phase", "blk"),
                P("phase", "blk", None),
                P("phase", None),
            ),
            out_specs=P("phase", None, "blk", None),
            check_vma=False,
        )(tokens, norm_gain, up_weight, up_bias, down_weight, down_bias)

    return whole
```

```python
import functools

import jax
import jax.numpy as jnp
from jax import lax
from jax.experimental import pallas as pl
from jax.experimental.pallas import tpu as pltpu
from jax.sharding import PartitionSpec as P

AXES = ("phase", "blk")
HBM = pl.BlockSpec(memory_space=pltpu.HBM)
VMEM = pl.BlockSpec(memory_space=pltpu.VMEM)
MIB = 1 << 20
SLOTS = 3
SUB = 512
CUT = 384
STRIP = 256
AHEAD = 1


def from_behind(block, axis, distance):
    devices = range(lax.axis_size(axis))
    route = [(i - distance, i) for i in devices if i - distance in devices]
    return lax.ppermute(block, axis, route)


def plain(tokens, norm_gain, up_weight, up_bias, down_weight, down_bias):
    num_micro, num_rows, width = tokens.shape
    phase_index = lax.axis_index("phase")
    num_phases = lax.axis_size("phase")
    inputs = tokens.reshape(num_micro * num_rows, width)
    result = inputs
    for moment in range(num_phases):
        if moment:
            inputs = from_behind(inputs, "phase", 1)
        widened = inputs.astype(jnp.float32)
        centered = widened - jnp.mean(widened, axis=-1, keepdims=True)
        row_var = jnp.mean(centered * centered, axis=-1, keepdims=True)
        normed = (centered * lax.rsqrt(row_var + 1e-05) * norm_gain[0]).astype(jnp.bfloat16)
        gathered = lax.all_gather(normed, "blk", axis=0, tiled=True)
        hidden = jnp.dot(gathered, up_weight[0], preferred_element_type=jnp.float32)
        hidden = jax.nn.gelu(hidden + up_bias[0]).astype(jnp.bfloat16)
        partial = jnp.dot(hidden, down_weight[0], preferred_element_type=jnp.float32)
        branch = lax.psum_scatter(
            partial.astype(jnp.bfloat16), "blk", scatter_dimension=0, tiled=True
        ).astype(jnp.float32)
        inputs = (widened + branch + down_bias[0]).astype(jnp.bfloat16)
        result = jnp.where(phase_index == moment, inputs, result)
    return result.reshape(1, num_micro, num_rows, width)


def near(*arrays):
    return [pltpu.with_memory_space_constraint(array, pltpu.VMEM) for array in arrays]


def far(array):
    return pltpu.with_memory_space_constraint(array, pltpu.HBM)


def call(kernel, operands, specs, shapes, scratch, megabytes, flops, moved):
    return pl.pallas_call(
        kernel,
        out_shape=shapes,
        in_specs=specs,
        out_specs=[VMEM] * len(shapes),
        scratch_shapes=scratch,
        compiler_params=pltpu.CompilerParams(vmem_limit_bytes=megabytes * MIB),
        cost_estimate=pl.CostEstimate(flops=flops, bytes_accessed=moved, transcendentals=0),
    )(*operands)


def part_of(index, size):
    return pl.ds(pl.multiple_of(index * size, size), size)


def fetch_kernel(n, w_down, *refs):
    kept, sems = refs[:n], refs[n]
    me = lax.axis_index("blk")
    copies = [
        pltpu.make_async_copy(
            w_down.at[0, :, part_of(me ^ order(i, n), kept[i].shape[1])], kept[i], sems.at[i]
        )
        for i in range(n)
    ]
    for copy in copies:
        copy.start()
    for copy in copies:
        copy.wait()


def fetch(n, w_down):
    depth, width = w_down.shape[1:]
    return call(
        functools.partial(fetch_kernel, n),
        (far(w_down),),
        [HBM],
        [pltpu.VMEM((depth, width // n), w_down.dtype)] * n,
        [pltpu.SemaphoreType.DMA((n,))],
        1,
        0,
        2 * width * depth,
    )


def first_kernel(n, *refs):
    blocks = refs[:n]
    gain, b_up, w_up, hidden, own, x, normed, ring, sems = refs[n:]
    me = lax.axis_index("blk")
    rows, width = x.shape
    group = rows // n
    parts = hidden.shape[1] // STRIP

    def weight_copy(i):
        slot = lax.rem(i, SLOTS)
        return pltpu.make_async_copy(
            w_up.at[0, :, part_of(i, STRIP)], ring.at[slot], sems.at[slot]
        )

    @pl.when(lax.axis_index("phase") == 0)
    def _():
        for i in range(SLOTS):
            weight_copy(jnp.int32(i)).start()
        for i in range(n):
            x[part_of(me ^ order(i, n), group)] = blocks[i][...]
        own[...] = x[:, part_of(me, own.shape[1])]

        @pl.loop(0, rows // 16)
        def _(i):
            part = part_of(i, 16)
            wide = x[part].astype(jnp.float32)
            centered = wide - jnp.mean(wide, axis=-1, keepdims=True)
            var = jnp.mean(centered * centered, axis=-1, keepdims=True)
            scaled = centered * lax.rsqrt(var + 1e-05) * gain[...]
            normed[part] = scaled.astype(jnp.bfloat16)

        @pl.loop(0, parts)
        def _(i):
            weight_copy(i).wait()
            part = part_of(i, STRIP)
            product = jnp.dot(
                normed[...], ring[lax.rem(i, SLOTS)], preferred_element_type=jnp.float32
            )
            hidden[:, part] = jax.nn.gelu(product + b_up[:, part]).astype(jnp.bfloat16)

            @pl.when(i + SLOTS < parts)
            def _():
                weight_copy(i + SLOTS).start()


def first_hidden(n, blocks, gain, b_up, w_up):
    width, depth = w_up.shape[1:]
    rows = blocks[0].shape[0] * n
    return call(
        functools.partial(first_kernel, n),
        (*near(*blocks, gain, b_up), far(w_up)),
        [VMEM] * (n + 2) + [HBM],
        [
            pltpu.VMEM((rows, depth), jnp.bfloat16),
            pltpu.VMEM((rows, width // n), jnp.bfloat16),
        ],
        [
            pltpu.VMEM((rows, width), jnp.bfloat16),
            pltpu.VMEM((rows, width), jnp.bfloat16),
            pltpu.VMEM((SLOTS, width, STRIP), jnp.bfloat16),
            pltpu.SemaphoreType.DMA((SLOTS,)),
        ],
        13,
        2 * rows * width * depth,
        2 * width * depth,
    )


def weight_copies(first, n, w_up, targets, sems):
    me = lax.axis_index("blk")
    chunk = targets[0].shape[0]
    cuts = chunk // CUT
    return [
        pltpu.make_async_copy(
            w_up.at[0, part_of((me ^ arrival(first + i, n)) * cuts + t, CUT)],
            target.at[pl.ds(t * CUT, CUT)],
            sems.at[i * cuts + t],
        )
        for i, target in enumerate(targets)
        for t in range(cuts)
    ]


def ahead_kernel(stage, n, w_up, *refs):
    *targets, sems = refs

    @pl.when(lax.axis_index("phase") == stage)
    def _():
        copies = weight_copies(0, n, w_up, targets, sems)
        for copy in copies:
            copy.start()
        for copy in copies:
            copy.wait()


def ahead(stage, n, w_up):
    width, depth = w_up.shape[1:]
    chunk = width // n
    return call(
        functools.partial(ahead_kernel, stage, n),
        (far(w_up),),
        [HBM],
        [pltpu.VMEM((chunk, depth), w_up.dtype)] * AHEAD,
        [pltpu.SemaphoreType.DMA((AHEAD * chunk // CUT,))],
        1,
        0,
        2 * AHEAD * chunk * depth,
    )


def up_kernel(stage, i, n, *refs):
    refs = list(refs)
    take = lambda length: [refs.pop(0) for _ in range(length)]
    first, last = i == 0, i == n - 1
    block, gain, weights = take(3)
    before, seen = (None, None) if first else take(2)
    fetches = i + AHEAD < n
    b_up = take(1)[0] if last else None
    w_up = take(1)[0] if fetches else None
    if last:
        hidden, scaled = refs
    else:
        total, noted, *refs = refs
        following = refs[:1] if fetches else []
        scaled = refs[len(following)]
    rows, chunk = block.shape
    depth = weights.shape[1]

    @pl.when(lax.axis_index("phase") == stage)
    def _():
        copies = weight_copies(i + AHEAD, n, w_up, following, refs[-1]) if fetches else []
        for copy in copies:
            copy.start()
        row = gain[:, part_of(lax.axis_index("blk") ^ arrival(i, n), chunk)]
        wide = block[...].astype(jnp.float32)
        shift = jnp.mean(wide, axis=-1, keepdims=True) if first else seen[0, :, :1]
        moved = wide - shift
        scaled[:rows] = (moved * row).astype(jnp.bfloat16)
        scaled[rows:] = jnp.broadcast_to(row, (16, chunk)).astype(jnp.bfloat16)
        one = jnp.sum(moved, axis=-1, keepdims=True)
        two = jnp.sum(moved * moved, axis=-1, keepdims=True)
        if not first:
            one = one + seen[1, :, :1]
            two = two + seen[2, :, :1]
        if not last:
            for t, value in enumerate((shift, one, two)):
                noted[t] = jnp.broadcast_to(value, (rows, 128))
        mean = one / (n * chunk)
        scale = lax.rsqrt(two / (n * chunk) - mean * mean + 1e-05)

        @pl.loop(0, depth // SUB, unroll=3)
        def _(c):
            part = part_of(c, SUB)
            product = jnp.dot(scaled[...], weights[:, part], preferred_element_type=jnp.float32)
            if not first:
                product = before[:, part] + product
            if last:
                product = (product[:rows] - mean * product[rows : rows + 1]) * scale
                hidden[:, part] = jax.nn.gelu(product + b_up[:, part]).astype(jnp.bfloat16)
            else:
                total[:, part] = product

        for copy in copies:
            copy.wait()


def next_hidden(stage, n, blocks, gain, b_up, w_up, weights):
    depth = w_up.shape[2]
    rows, chunk = blocks[0].shape
    total = (rows + 16, depth)
    carried = []
    for i in range(n):
        last, fetches = i == n - 1, i + AHEAD < n
        operands = near(blocks[i], gain, weights[i], *carried, *([b_up] if last else []))
        results = call(
            functools.partial(up_kernel, stage, i, n),
            [*operands, far(w_up)] if fetches else operands,
            [VMEM] * len(operands) + [HBM] * fetches,
            [pltpu.VMEM((rows, depth), jnp.bfloat16)]
            if last
            else [
                pltpu.VMEM(total, jnp.float32),
                pltpu.VMEM((3, rows, 128), jnp.float32),
                *[pltpu.VMEM((chunk, depth), jnp.bfloat16)] * fetches,
            ],
            [pltpu.VMEM((rows + 16, chunk), jnp.bfloat16)]
            + [pltpu.SemaphoreType.DMA((chunk // CUT,))] * fetches,
            3,
            2 * rows * chunk * depth,
            2 * chunk * depth,
        )
        carried = results[:2]
        weights = [*weights, *results[2:]]
    return results[0]


def down_kernel(stage, hidden, weights, *refs):
    sent = refs[-1]

    @pl.when(lax.axis_index("phase") == stage)
    def _():
        product = jnp.dot(hidden[...], weights[...], preferred_element_type=jnp.float32)
        if len(refs) > 1:
            x, b_down, _ = refs
            columns = part_of(lax.axis_index("blk"), sent.shape[1])
            product = product + x[...].astype(jnp.float32) + b_down[:, columns]
        sent[...] = product.astype(jnp.bfloat16)


def down(stage, hidden, weights, own, b_down):
    rows, depth = hidden.shape
    chunk = weights.shape[1]
    operands = [hidden, weights] + ([] if own is None else [own, b_down])
    return call(
        functools.partial(down_kernel, stage),
        near(*operands),
        [VMEM] * len(operands),
        [pltpu.VMEM((rows, chunk), jnp.bfloat16)],
        [],
        2,
        2 * rows * depth,
        2 * depth,
    )[0]


def last_kernel(stage, n, hidden, x, b_down, *refs):
    weights, sent, whole = refs[:n], refs[n : 2 * n], refs[2 * n]
    me = lax.axis_index("blk")
    chunk = weights[0].shape[1]
    group = x.shape[0]

    @pl.when(lax.axis_index("phase") == stage)
    def _():
        for i in range(n):
            product = jnp.dot(hidden[...], weights[i][...], preferred_element_type=jnp.float32)
            whole[:, part_of(me ^ order(i, n), chunk)] = product.astype(jnp.bfloat16)
        for i in range(n):
            part = whole[part_of(me ^ order(i, n), group)]
            if order(i, n) == 0:
                part = part.astype(jnp.float32) + x[...].astype(jnp.float32) + b_down[...]
            sent[i][...] = part.astype(jnp.bfloat16)


def last_down(stage, n, hidden, down_kept, own, b_down):
    rows, depth = hidden.shape
    group, width = own.shape
    return call(
        functools.partial(last_kernel, stage, n),
        near(hidden, own, b_down, *down_kept),
        [VMEM] * (n + 3),
        [pltpu.VMEM((group, width), jnp.bfloat16)] * n,
        [pltpu.VMEM((rows, width), jnp.bfloat16)],
        4,
        2 * rows * depth * width,
        2 * depth * width,
    )


def rows_kernel(stage, n, *refs):
    blocks, own = refs[:n], refs[-1]
    me = lax.axis_index("blk")
    group = own.shape[0]
    chunk = blocks[0].shape[1]

    if stage > 1:

        @pl.when(lax.axis_index("phase") != stage)
        def _():
            own[...] = refs[n][...]

    @pl.when(lax.axis_index("phase") == stage)
    def _():
        for i in range(n):
            own[:, part_of(me ^ arrival(i, n), chunk)] = blocks[i][part_of(me, group)]


def own_rows(stage, n, blocks, kept):
    rows, chunk = blocks[0].shape
    operands = [*blocks] + ([kept] if stage > 1 else [])
    return call(
        functools.partial(rows_kernel, stage, n),
        near(*operands),
        [VMEM] * len(operands),
        [pltpu.VMEM((rows // n, chunk * n), jnp.bfloat16)],
        [],
        1,
        0,
        4 * rows * chunk,
    )[0]


def order(i, n):
    half = n // 2
    return (i + 1) // 2 % half if i % 2 else i // 2 + half


def arrival(i, n):
    half = n // 2
    return (0, 1, half, half + 1)[i] if i < 4 else i // 2 + (half if i % 2 else 0)


def send(block, source, target, step, n, phases):
    pairs = ((source, target),)
    if source ^ 1 == target:
        pairs = [(p, p ^ 1) for p in range(source % 2, phases, 2)]
    return lax.ppermute(block, AXES, [(p * n + b, q * n + (b ^ step)) for p, q in pairs for b in range(n)])


def relay(tokens, norm_gain, up_weight, up_bias, down_weight, down_bias):
    num_micro, num_rows, width = tokens.shape
    n = lax.axis_size("blk")
    num_phases = lax.axis_size("phase")
    phase = lax.axis_index("phase")
    steps = [order(i, n) for i in range(n)]
    mine = tokens.reshape(num_micro * num_rows, width)
    blocks = [order(i, n) for i in range(n)]
    blocks = [send(mine, 1, 0, step, n, num_phases) if step else mine for step in blocks]
    down_kept = fetch(n, down_weight)
    kept = None
    for stage in range(num_phases):
        last = stage == num_phases - 1
        adder = stage ^ 1
        turns = [*range(n)]
        if stage == 0:
            turns[3 : n - 1] = [i for k in range(4, n - 1, 2) for i in (k, k - 1)]
            turns = [*turns[4 : n - 1], *turns[:4], n - 1]
        if stage == 0:
            hidden, own = first_hidden(n, blocks, norm_gain, up_bias, up_weight)
        else:
            hidden = next_hidden(stage, n, blocks, norm_gain, up_bias, up_weight, early)
            kept = own_rows(stage, n, blocks, kept)
            own = blocks[0]
        if last:
            sent = last_down(stage, n, hidden, down_kept, kept, down_bias)
        else:
            sent = [
                down(stage, hidden, down_kept[i], None if steps[i] else own, down_bias)
                for i in turns
            ]
        landed = [send(sent[k], stage, adder, steps[i], n, num_phases) for k, i in enumerate(turns)]
        total = landed[0].astype(jnp.float32)
        for block in landed[1:]:
            total = total + block.astype(jnp.float32)
        total = total.astype(jnp.bfloat16)
        if not last:
            own = total if adder == stage + 1 else send(total, adder, stage + 1, 0, n, num_phases)
            sender = (stage + 1) ^ 1
            total = send(total, adder, sender, 0, n, num_phases)
            early = ahead(stage + 1, n, up_weight)
            blocks = {step: send(total, sender, stage + 1, step, n, num_phases) for step in steps if step}
            blocks[0] = own
            blocks = [blocks[arrival(i, n)] for i in range(n)]
    straight = send(kept, 1, 0, 0, n, num_phases)
    across = send(kept, 2, 1, 0, n, num_phases)
    final = send(total, adder, stage, 0, n, num_phases)
    result = jnp.where(phase == stage, final, jnp.where(phase == 1, across, straight))
    return result.reshape(1, num_micro, num_rows, width)


def fits(mesh, tokens, up_weight):
    n = mesh.shape["blk"]
    num_micro, num_tokens, width = tokens.shape
    depth = up_weight.shape[2] // n
    rows = num_micro * num_tokens
    chunk = width // n
    chunk = width // n
    return (
        mesh.shape["phase"] == 4
        and n & (n - 1) == 0
        and n >= 4
        and chunk % CUT == 0
        and depth % SUB == 0
        and depth % STRIP == 0
        and (rows // n) % 16 == 0
        and 2 * depth * (width + (AHEAD + 1) * chunk) <= 50 * MIB
        and 4 * rows * width + 2 * SLOTS * width * STRIP <= 12 * MIB
        and 4 * rows * depth <= 2 * MIB
    )


def solution(mesh):
    def whole(tokens, norm_gain, up_weight, up_bias, down_weight, down_bias):
        body = relay if fits(mesh, tokens, up_weight) else plain
        return jax.shard_map(
            body,
            mesh=mesh,
            in_specs=(
                P(None, "blk", None),
                P("phase", None),
                P("phase", None, "blk"),
                P("phase", "blk"),
                P("phase", "blk", None),
                P("phase", None),
            ),
            out_specs=P("phase", None, "blk", None),
            check_vma=False,
        )(tokens, norm_gain, up_weight, up_bias, down_weight, down_bias)

    return whole
```
